32 devices in a mesh: mom: 2 (over x), en: 16 (over z, y, core).
Axes of the slice: x: 2, y: 2, z: 4, core: 2. Of those that a mesh axis runs over, the one named last changes fastest.
Arguments:
- green0: bfloat16 [2, 64, 2, 512, 512], P('mom', 'en'), may hold values from -6 to 6
- phonon_me: bfloat16 [512, 512], replicated, may hold values from 0.25 to 4
- coupling: float32 [2, 2, 16], replicated, may hold values from 0.0015 to 0.045
- shift_table: int32 [2, 16], replicated, may hold values from 0 to 1
- offsets: int32 [16], replicated, may hold values from 1 to 8
Outputs:
- green: bfloat16 [2, 64, 2, 512, 512], P('mom', 'en')
The draws below stay inside these ranges and needn't reach their ends.
All inputs are finite; a program needn't handle non-finite values.
Results may differ from the reference program's by a relative error of at most 0.02.
Values may be sent and summed in bfloat16 or wider, within the bound.
No kernel may reach another device: no remote copies, remote signals or barrier semaphores. Data moves between devices by JAX's collectives and lax.ppermute only.
A program may use at most 128 MiB of HBM per device.

```python
import math
import jax
import jax.numpy as jnp
from jax import lax

NORB = 512
NW = 16
NEUMANN = 3
NK = 2
NE = 64


def plant(values, stream_key, least, largest):
    place = [jax.random.randint(jax.random.fold_in(stream_key, axis), (), 0, length) for axis, length in enumerate(values.shape)]
    main_axis = values.shape.index(max(values.shape))
    beside = place[:main_axis] + [(place[main_axis] + 1) % values.shape[main_axis]] + place[main_axis + 1:]
    return values.at[tuple(place)].set(least).at[tuple(beside)].set(largest)


def block_scale(key, extent, shards, least, largest):
    def one(dim, parts):
        steps = jax.random.uniform(jax.random.fold_in(jax.random.fold_in(key, 6), dim), (parts,), jnp.float32, least / len(shards), largest / len(shards))
        return jnp.repeat(jnp.exp(steps), extent[dim] // parts).reshape((-1,) + (1,) * (len(extent) - dim - 1))

    gain = one(*shards[0])
    for cut in shards[1:]:
        gain = gain * one(*cut)
    return gain


def bell_draw(rng, extent, scale, limit, split=(), held_as=jnp.bfloat16):
    values = scale * jax.random.normal(rng, extent, jnp.float32)
    if split:
        values = values * block_scale(rng, extent, split, -0.22, 0.18)
    return jnp.clip(values, -limit, limit).astype(held_as)


def setup_inputs(seed: int = 0) -> dict:
    key_of = jax.random.split(jax.random.key(seed), 6)
    return {
        "green0": bell_draw(key_of[0], (NK, NE, 2, NORB, NORB), 1.0, 6.0, ((0, 2), (1, 16))),
        "phonon_me": jnp.clip(jnp.exp(jax.random.uniform(key_of[1], (NORB, NORB), jnp.float32, math.log(0.25), math.log(4.0))), 0.25, 4.0).astype(jnp.bfloat16),
        "coupling": jnp.clip(jnp.exp(jax.random.uniform(key_of[2], (2, NK, NW), jnp.float32, math.log(0.0015), math.log(0.045))), 0.0015, 0.045),
        "shift_table": plant(jax.random.randint(key_of[3], (NK, NW), 0, NK), jax.random.fold_in(key_of[3], 1), 0, NK - 1).astype(jnp.int32),
        "offsets": plant(jax.random.randint(key_of[4], (NW,), 1, NE // 8 + 1), jax.random.fold_in(key_of[4], 1), 1, (NE // 8 + 1) - 1).astype(jnp.int32),
    }


def kernel_table(shift_table, coupling, offsets):
    energy = jnp.arange(NE, dtype=jnp.int32)
    offset_grid = energy[:, None] - energy[None, :]
    downward = (offset_grid[None, :, :] == offsets[:, None, None]).astype(jnp.float32)
    upward = (offset_grid[None, :, :] == -offsets[:, None, None]).astype(jnp.float32)
    moment = jnp.arange(NK, dtype=jnp.int32)
    select = (shift_table[:, :, None] == moment[None, None, :]).astype(jnp.float32)
    emission = jnp.einsum('awb,aw->abw', select, coupling[0].astype(jnp.float32))
    absorption = jnp.einsum('awb,aw->abw', select, coupling[1].astype(jnp.float32))
    kernel = jnp.einsum('abw,wef->abef', emission, downward) + jnp.einsum('abw,wef->abef', absorption, upward)
    return kernel.astype(jnp.bfloat16)


def reference(green0, phonon_me, coupling, shift_table, offsets):
    kernel = kernel_table(shift_table, coupling, offsets)
    green_wide = green0.astype(jnp.float32).reshape(NK, NE, 2 * NORB * NORB)
    scale = 1.0 / NORB

    def dyson(operands):
        green_in, smooth = operands
        self_energy = (phonon_me.astype(jnp.float32) * smooth.astype(jnp.float32)).astype(jnp.bfloat16)
        left_factor = jnp.concatenate([green_in[0], green_in[1]], axis=1)
        right_real = jnp.concatenate([self_energy[0], -self_energy[1]], axis=0)
        right_imag = jnp.concatenate([self_energy[1], self_energy[0]], axis=0)
        prod_real = (jnp.dot(left_factor, right_real, preferred_element_type=jnp.float32) * scale).astype(jnp.bfloat16)
        prod_imag = (jnp.dot(left_factor, right_imag, preferred_element_type=jnp.float32) * scale).astype(jnp.bfloat16)
        transfer = jnp.concatenate([prod_real, prod_imag], axis=1)
        current_real = green_in[0]
        current_imag = green_in[1]
        for iteration in range(NEUMANN):
            stacked_real = jnp.concatenate([current_real, -current_imag], axis=0)
            stacked_imag = jnp.concatenate([current_imag, current_real], axis=0)
            new_real = green_in[0].astype(jnp.float32) + jnp.dot(transfer, stacked_real, preferred_element_type=jnp.float32)
            new_imag = green_in[1].astype(jnp.float32) + jnp.dot(transfer, stacked_imag, preferred_element_type=jnp.float32)
            current_real = new_real.astype(jnp.bfloat16)
            current_imag = new_imag.astype(jnp.bfloat16)
        return jnp.stack([current_real, current_imag], axis=0)

    outputs = []
    for target in range(NK):
        smooth = jnp.einsum('bef,bfx->ex', kernel[target].astype(jnp.float32), green_wide)
        smooth = smooth.astype(jnp.bfloat16).reshape(NE, 2, NORB, NORB)
        outputs.append(lax.map(dyson, (green0[target], smooth)))
    return jnp.stack(outputs, axis=0)
```

```python
import functools

import jax
import jax.numpy as jnp
from jax import lax
from jax.experimental import pallas as pl
from jax.experimental.pallas import tpu as pltpu
from jax.sharding import PartitionSpec as P

NEUMANN = 3
TILE = 16
AXES = ("mom", "en")
VMEM_LIMIT = 48 * 1024 * 1024


class Place:
    def __init__(self, local_energies, orbitals):
        self.moms = lax.axis_size("mom")
        self.ens = lax.axis_size("en")
        self.local = local_energies
        self.energies = local_energies * self.ens
        self.reach = -(-(self.energies // 8) // local_energies)
        self.planes = self.ens // (2 * self.reach)
        assert self.planes * 2 * self.reach == self.ens
        self.group = self.moms * 2 * self.reach
        self.rows = orbitals // self.group
        self.shifts = [
            (dm, dh, dq)
            for dh in range(2)
            for dm in range(self.moms)
            for dq in range(self.reach)
        ]

    def here(self):
        n = lax.axis_index("en")
        plane = 2 * self.reach
        return lax.axis_index("mom"), n // plane, (n // self.reach) % 2, n % self.reach

    def index(self, m, z, h, q):
        return m * self.ens + (z * 2 + h) * self.reach + q

    def everyone(self):
        return [
            (m, z, h, q)
            for m in range(self.moms)
            for z in range(self.planes)
            for h in range(2)
            for q in range(self.reach)
        ]

    def target(self, m, h, q, shift):
        dm, dh, dq = shift
        return (m + dm) % self.moms, (h + dh) % 2, (q + dq) % self.reach

    def source(self, m, h, q, shift):
        dm, dh, dq = shift
        return (m - dm) % self.moms, (h + dh) % 2, (q - dq) % self.reach

    def tile(self, m, h, q):
        return (m * 2 + h) * self.reach + q

    def shift_perm(self, shift):
        pairs = []
        for m, z, h, q in self.everyone():
            tm, th, tq = self.target(m, h, q, shift)
            pairs.append((self.index(m, z, h, q), self.index(tm, z, th, tq)))
        return pairs

    def plane_perm(self, other):
        pairs = []
        for m, z, h, q in self.everyone():
            to = z + (1 if (h + other) % 2 == 1 else -1)
            if 0 <= to < self.planes:
                pairs.append((self.index(m, z, h, q), self.index(m, to, h, q)))
        return pairs

    def first_energy(self, z, h, q):
        return ((z * 2 + h) * self.reach + q) * self.local


def mixing(place, coupling, shift_table, offsets):
    m, z, h, q = place.here()
    source_mom, source_energy, target_mom, target_energy = [], [], [], []
    span = jnp.arange(place.local, dtype=jnp.int32)

    def add(moms, energies, mom, first):
        moms.append(jnp.full((place.local,), mom, jnp.int32))
        energies.append(first + span)

    for shift in place.shifts:
        tm, th, tq = place.target(m, h, q, shift)
        add(target_mom, target_energy, tm, place.first_energy(z, th, tq))
        sm, sh, sq = place.source(m, h, q, shift)
        add(source_mom, source_energy, sm, place.first_energy(z, sh, sq))
    for other in range(2):
        from_plane = jnp.where((h + other) % 2 == 1, z - 1, z + 1)
        for shift in place.shifts:
            if shift[1] == other:
                sm, sh, sq = place.source(m, h, q, shift)
                add(source_mom, source_energy, sm, place.first_energy(from_plane, sh, sq))
    source_mom, source_energy = jnp.concatenate(source_mom), jnp.concatenate(source_energy)
    target_mom, target_energy = jnp.concatenate(target_mom), jnp.concatenate(target_energy)
    one_hot = (target_mom[:, None] == jnp.arange(place.moms, dtype=jnp.int32)[None]).astype(jnp.float32)
    pick = functools.partial(jnp.einsum, "tm,mw->tw", one_hot, precision=lax.Precision.HIGHEST)
    emission, absorption = pick(coupling[0]), pick(coupling[1])
    shifted = jnp.sum(
        jnp.where(target_mom[:, None, None] == jnp.arange(place.moms)[None, :, None], shift_table[None], 0), axis=1
    )
    apart = (target_energy[:, None] - source_energy[None])[:, :, None]
    chosen = shifted[:, None, :] == source_mom[None, :, None]
    real = ((source_energy >= 0) & (source_energy < place.energies))[None, :, None]
    terms = jnp.where(apart == offsets, emission[:, None, :], 0.0) + jnp.where(
        apart == -offsets, absorption[:, None, :], 0.0
    )
    table = jnp.sum(jnp.where(chosen & real, terms, 0.0), axis=2).astype(jnp.bfloat16)
    targets, sources = table.shape
    tall = (jnp.arange(targets * TILE)[:, None] // TILE == jnp.arange(targets)[None]).astype(jnp.bfloat16)
    wide = (jnp.arange(sources)[:, None] == jnp.arange(sources * TILE)[None] // TILE).astype(jnp.bfloat16)
    spread = jnp.dot(tall, table, preferred_element_type=jnp.float32).astype(jnp.bfloat16)
    spread = jnp.dot(spread, wide, preferred_element_type=jnp.float32)
    diagonal = jnp.arange(targets * TILE)[:, None] % TILE == jnp.arange(sources * TILE)[None] % TILE
    return jnp.where(diagonal, spread, 0.0).astype(jnp.bfloat16)


def smooth_kernel(local, splits, n_in, place_ref, mix_ref, own_ref, *refs):
    pieces, halos, outs = refs[: n_in - 2], refs[n_in - 2 : n_in], refs[n_in:]
    width = own_ref.shape[-1]
    parts = [own_ref[0, :, 0].reshape(local * TILE, width)]
    parts += [r[...].reshape(local * TILE, width) for r in pieces]
    parts += [r[...].reshape(-1, width) for r in halos]
    stacked = jnp.concatenate(parts, axis=0)
    mixed = jnp.dot(mix_ref[...], stacked, preferred_element_type=jnp.float32).astype(jnp.bfloat16)
    at = 0
    for i, out in enumerate(outs):
        first, last = splits[i % len(splits)]
        out[...] = mixed[at : at + (last - first) * TILE].reshape(last - first, TILE, width)
        at += (last - first) * TILE


def smooth_call(place, part, green0, mix, pieces, halos, splits):
    local, orbitals = place.local, green0.shape[-1]
    steps = place.rows // TILE
    m, z, h, q = place.here()
    where = jnp.asarray(place.tile(m, h, q) * steps, jnp.int32).reshape(1)
    block = pl.BlockSpec((local, TILE, orbitals), lambda j, w: (0, j, 0))
    halo = halos[0].shape[0]
    return pl.pallas_call(
        functools.partial(smooth_kernel, local, splits, len(pieces) + 2),
        out_shape=[
            jax.ShapeDtypeStruct((last - first, place.rows, orbitals), jnp.bfloat16)
            for _ in place.shifts
            for first, last in splits
        ],
        grid_spec=pltpu.PrefetchScalarGridSpec(
            num_scalar_prefetch=1,
            grid=(steps,),
            in_specs=[
                pl.BlockSpec(mix.shape, lambda j, w: (0, 0)),
                pl.BlockSpec((1, local, 1, TILE, orbitals), lambda j, w: (0, 0, part, w[0] + j, 0)),
            ]
            + [block] * len(pieces)
            + [pl.BlockSpec((halo, TILE, orbitals), lambda j, w: (0, j, 0))] * 2,
            out_specs=[
                pl.BlockSpec((last - first, TILE, orbitals), lambda j, w: (0, j, 0))
                for _ in place.shifts
                for first, last in splits
            ],
        ),
        compiler_params=pltpu.CompilerParams(vmem_limit_bytes=VMEM_LIMIT),
        cost_estimate=pl.CostEstimate(
            flops=2 * mix.shape[0] * mix.shape[1] * steps * orbitals,
            bytes_accessed=2 * (mix.size + (mix.shape[0] + mix.shape[1]) * steps * orbitals),
            transcendentals=0,
        ),
        name="smooth",
    )(where, mix, green0, *pieces, *halos)


def dyson_kernel(rows, n, tile_ref, green_ref, phonon_ref, *refs):
    reals, imags = refs[:n], refs[n : 2 * n]
    out_ref, energy, transfer, series = refs[-4:]
    size = phonon_ref.shape[0]
    low, high = pl.ds(0, size), pl.ds(size, size)

    def put(to, re, im, at=None):
        top = low if at is None else pl.ds(at, rows)
        bottom = high if at is None else pl.ds(size + at, rows)
        to[top, low] = re
        to[bottom, high] = re
        to[top, high] = im
        to[bottom, low] = -im

    for k in range(n):
        at = pl.multiple_of(tile_ref[k] * rows, rows)
        scale = phonon_ref[pl.ds(at, rows), :].astype(jnp.float32)
        re = (scale * reals[k][0].astype(jnp.float32)).astype(jnp.bfloat16)
        im = (scale * imags[k][0].astype(jnp.float32)).astype(jnp.bfloat16)
        put(energy, re, im, at)
    left = jnp.concatenate([green_ref[0, 0, 0], green_ref[0, 0, 1]], axis=1)
    product = jnp.dot(left, energy[...], preferred_element_type=jnp.float32)
    transfer[...] = (product * (1.0 / size)).astype(jnp.bfloat16)
    put(series, green_ref[0, 0, 0], green_ref[0, 0, 1])
    for step in range(NEUMANN):
        added = left.astype(jnp.float32) + jnp.dot(
            transfer[...], series[...], preferred_element_type=jnp.float32
        )
        added = added.astype(jnp.bfloat16)
        if step < NEUMANN - 1:
            put(series, added[:, :size], added[:, size:])
        else:
            out_ref[0, 0, 0] = added[:, :size]
            out_ref[0, 0, 1] = added[:, size:]


def dyson_call(place, green0, phonon_me, reals, imags, first, last, out):
    size, rows, n = green0.shape[-1], place.rows, len(reals)
    m, z, h, q = place.here()
    tiles = jnp.stack([place.tile(*place.source(m, h, q, s)) for s in place.shifts]).astype(jnp.int32)
    block = pl.BlockSpec((1, 1, 2, size, size), lambda e, t: (0, first + e, 0, 0, 0))
    piece = pl.BlockSpec((1, rows, size), lambda e, t: (first + e, 0, 0))
    late = pl.BlockSpec((1, rows, size), lambda e, t: (e, 0, 0))
    specs = [block, pl.BlockSpec((size, size), lambda e, t: (0, 0))] + [piece] * n + [late] * n
    args = [tiles, green0, phonon_me, *reals, *imags]
    aliases = {}
    if out is not None:
        aliases = {len(args): 0}
        args.append(out)
        specs.append(pl.BlockSpec(memory_space=pl.ANY))
    count = last - first
    return pl.pallas_call(
        functools.partial(dyson_kernel, rows, n),
        out_shape=jax.ShapeDtypeStruct(green0.shape, green0.dtype),
        grid_spec=pltpu.PrefetchScalarGridSpec(
            num_scalar_prefetch=1,
            grid=(count,),
            in_specs=specs,
            out_specs=block,
            scratch_shapes=[
                pltpu.VMEM((2 * size, 2 * size), jnp.bfloat16),
                pltpu.VMEM((size, 2 * size), jnp.bfloat16),
                pltpu.VMEM((2 * size, 2 * size), jnp.bfloat16),
            ],
        ),
        input_output_aliases=aliases,
        compiler_params=pltpu.CompilerParams(vmem_limit_bytes=VMEM_LIMIT),
        cost_estimate=pl.CostEstimate(
            flops=count * (NEUMANN + 1) * 8 * size**3,
            bytes_accessed=(6 * count + 1) * 2 * size * size,
            transcendentals=0,
        ),
        name="dyson",
    )(*args)


def per_device(green0, phonon_me, coupling, shift_table, offsets):
    local, orbitals = green0.shape[1], green0.shape[3]
    place = Place(local, orbitals)
    m, z, h, q = place.here()
    mix = mixing(place, coupling, shift_table, offsets)
    splits = ((0, local // 2), (local // 2, local))
    whole = ((0, local),)
    pieces = [[], []]
    for part in range(2):
        for shift in place.shifts:
            at = place.tile(*place.target(m, h, q, shift)) * place.rows
            piece = lax.dynamic_slice(
                green0, (0, 0, part, at, 0), (1, local, 1, place.rows, orbitals)
            ).reshape(local, place.rows, orbitals)
            if shift != (0, 0, 0):
                piece = lax.ppermute(piece, AXES, place.shift_perm(shift))
            pieces[part].append(piece)
    back = []
    half = place.group // 2
    for part in range(2):
        halos = [
            lax.ppermute(
                jnp.concatenate(pieces[part][other * half : (other + 1) * half], axis=0),
                AXES,
                place.plane_perm(other),
            )
            for other in range(2)
        ]
        cut = whole if part == 0 else splits
        mixed = smooth_call(place, part, green0, mix, pieces[part][1:], halos, cut)
        arrived = []
        for s in range(len(cut)):
            arrived.append(
                [
                    mixed[i * len(cut) + s]
                    if shift == (0, 0, 0)
                    else lax.ppermute(mixed[i * len(cut) + s], AXES, place.shift_perm(shift))
                    for i, shift in enumerate(place.shifts)
                ]
            )
        back.append(arrived)
    out = None
    for s, (first, last) in enumerate(splits):
        out = dyson_call(place, green0, phonon_me, back[0][0], back[1][s], first, last, out)
    return out


def solution(mesh):
    in_specs = (P("mom", "en", None, None, None), P(), P(), P(), P())
    out_specs = P("mom", "en", None, None, None)
    return jax.shard_map(
        per_device, mesh=mesh, in_specs=in_specs, out_specs=out_specs, check_vma=False
    )
```

```python
import functools

import jax
import jax.numpy as jnp
from jax import lax
from jax.experimental import pallas as pl
from jax.experimental.pallas import tpu as pltpu
from jax.sharding import PartitionSpec as P

NEUMANN = 3
TILE = 16
STEP = 32
CUTS = 2
AXES = ("mom", "en")
SMALL_VMEM = 12 * 1024 * 1024
VMEM_LIMIT = 20 * 1024 * 1024


class Place:
    def __init__(self, local_energies, orbitals):
        self.moms = lax.axis_size("mom")
        self.ens = lax.axis_size("en")
        self.local = local_energies
        self.energies = local_energies * self.ens
        self.reach = -(-(self.energies // 8) // local_energies)
        self.planes = self.ens // (2 * self.reach)
        assert self.planes * 2 * self.reach == self.ens
        self.block = 2 * orbitals // (2 * self.moms)
        units = self.block // STEP
        assert units * STEP == self.block
        sizes = [STEP * (units // CUTS + (i < units % CUTS)) for i in range(CUTS)]
        self.parts = [(sum(sizes[:i]), size) for i, size in enumerate(sizes) if size]
        self.shifts = [(dm, dh) for dh in range(2) for dm in range(self.moms)]

    def here(self):
        n = lax.axis_index("en")
        plane = 2 * self.reach
        return lax.axis_index("mom"), n // plane, (n // self.reach) % 2, n % self.reach

    def index(self, m, z, h, q):
        return m * self.ens + (z * 2 + h) * self.reach + q

    def everyone(self):
        return [
            (m, z, h, q)
            for m in range(self.moms)
            for z in range(self.planes)
            for h in range(2)
            for q in range(self.reach)
        ]

    def target(self, m, h, shift):
        return (m + shift[0]) % self.moms, (h + shift[1]) % 2

    def source(self, m, h, shift):
        return (m - shift[0]) % self.moms, (h + shift[1]) % 2

    def row(self, m, h, part):
        return (m * 2 + h) * self.block + part[0]

    def shift_perm(self, shift):
        pairs = []
        for m, z, h, q in self.everyone():
            tm, th = self.target(m, h, shift)
            pairs.append((self.index(m, z, h, q), self.index(tm, z, th, q)))
        return pairs

    def goes_up(self, z, odd):
        return z % 2 == odd

    def plane_perm(self, odd):
        pairs = []
        for m, z, h, q in self.everyone():
            to = z + 1 if self.goes_up(z, odd) else z - 1
            if 0 <= to < self.planes:
                pairs.append((self.index(m, z, h, q), self.index(m, to, h, q)))
        return pairs

    def swap_perm(self, dq):
        return [
            (self.index(m, z, h, q), self.index(m, z, h, (q + dq) % self.reach))
            for m, z, h, q in self.everyone()
        ]

    def first_energy(self, z, h, q):
        return ((z * 2 + h) * self.reach + q) * self.local


def mix_kernel(place, coupling_ref, shift_ref, offset_ref, here_ref, *outs):
    m, z, h, q = here_ref[0], here_ref[1], here_ref[2], here_ref[3]
    count = len(place.shifts) * place.local
    shape = (place.reach * count, 2 * count)
    row = lax.broadcasted_iota(jnp.int32, shape, 0)
    column = lax.broadcasted_iota(jnp.int32, shape, 1)

    def energy(plane, half, at, of):
        return ((plane * 2 + half) * place.reach + at) * place.local + of % place.local

    shift = (row // place.local) % len(place.shifts)
    target_mom = (m + shift % place.moms) % place.moms
    target_energy = energy(z, (h + shift // place.moms) % 2, (q + row // count) % place.reach, row)
    shift = (column // place.local) % len(place.shifts)
    second = shift // place.moms
    up = (z + second) % 2 == 0
    near = column < count
    plane = jnp.where(near, z, jnp.where(up, z + 1, z - 1))
    half = jnp.where(near, (h + second) % 2, jnp.where(up, 0, 1))
    source_mom = (m + place.moms - shift % place.moms) % place.moms
    source_energy = energy(plane, half, q, column)
    real = (source_energy >= 0) & (source_energy < place.energies)
    apart = jnp.where(real, target_energy - source_energy, 2 * place.energies)
    table = jnp.zeros(shape, jnp.float32)
    for k in range(place.moms):
        here = target_mom == k
        for w in range(offset_ref.shape[0]):
            chosen = here & (source_mom == shift_ref[k, w])
            table += jnp.where(chosen & (apart == offset_ref[w]), coupling_ref[0, k, w], 0.0)
            table += jnp.where(chosen & (apart == -offset_ref[w]), coupling_ref[1, k, w], 0.0)
    table = table.astype(jnp.bfloat16)
    wide = (2 * count, 2 * count * TILE)
    spread = (
        lax.broadcasted_iota(jnp.int32, wide, 0) == lax.broadcasted_iota(jnp.int32, wide, 1) // TILE
    ).astype(jnp.bfloat16)
    tall = (count * TILE, count)
    repeat = (
        lax.broadcasted_iota(jnp.int32, tall, 0) // TILE == lax.broadcasted_iota(jnp.int32, tall, 1)
    ).astype(jnp.bfloat16)
    full = (count * TILE, 2 * count * TILE)
    diagonal = lax.broadcasted_iota(jnp.int32, full, 0) % TILE == lax.broadcasted_iota(jnp.int32, full, 1) % TILE
    for dq, out in enumerate(outs):
        part = table[dq * count : (dq + 1) * count]
        part = jnp.dot(part, spread, preferred_element_type=jnp.float32).astype(jnp.bfloat16)
        part = jnp.dot(repeat, part, preferred_element_type=jnp.float32)
        out[...] = jnp.where(diagonal, part, 0.0).astype(jnp.bfloat16)


def mixing(place, coupling, shift_table, offsets, after):
    count = len(place.shifts) * place.local
    shape = (count * TILE, 2 * count * TILE)
    smem = pl.BlockSpec(memory_space=pltpu.SMEM)

    def kernel(coupling_ref, shift_ref, offset_ref, here_ref, *refs):
        mix_kernel(place, coupling_ref, shift_ref, offset_ref, here_ref, *refs[len(after) :])

    return pl.pallas_call(
        kernel,
        out_shape=[jax.ShapeDtypeStruct(shape, jnp.bfloat16)] * place.reach,
        in_specs=[smem] * 4 + anywhere(after),
        out_specs=[in_vmem()] * place.reach,
        compiler_params=pltpu.CompilerParams(vmem_limit_bytes=2 * SMALL_VMEM),
        cost_estimate=pl.CostEstimate(flops=0, bytes_accessed=0, transcendentals=0),
        name="mixing",
    )(coupling, shift_table, offsets, jnp.stack(place.here()).astype(jnp.int32), *after)


def in_vmem():
    return pl.BlockSpec(memory_space=pltpu.VMEM)


def in_hbm(x):
    return pltpu.with_memory_space_constraint(x, pltpu.HBM)


def anywhere(arrays):
    return [pl.BlockSpec(memory_space=pl.ANY)] * len(arrays)


def cut_kernel(n, sizes, at_ref, green_ref, *refs):
    outs, sems = refs[-n - 1 : -1], refs[-1]
    copies = []
    for k, out in enumerate(outs):
        rows = pl.ds(pl.multiple_of(at_ref[k], STEP), sizes)
        copies.append(pltpu.make_async_copy(green_ref.at[0, :, rows, :], out, sems.at[k]))
    for copy in copies:
        copy.start()
    for copy in copies:
        copy.wait()


def cut_call(place, part, green0, after):
    local, orbitals = place.local, green0.shape[-1]
    m, z, h, q = place.here()
    at = jnp.stack([place.row(*place.target(m, h, shift), part) for shift in place.shifts]).astype(jnp.int32)
    shape = (local, part[1], orbitals)
    n = len(place.shifts)
    return pl.pallas_call(
        functools.partial(cut_kernel, n, part[1]),
        out_shape=[jax.ShapeDtypeStruct(shape, jnp.bfloat16)] * n,
        in_specs=[pl.BlockSpec(memory_space=pltpu.SMEM)] + anywhere([green0, *after]),
        out_specs=[in_vmem()] * n,
        scratch_shapes=[pltpu.SemaphoreType.DMA((n,))],
        compiler_params=pltpu.CompilerParams(vmem_limit_bytes=SMALL_VMEM),
        cost_estimate=pl.CostEstimate(flops=0, bytes_accessed=0, transcendentals=0),
        name="cut",
    )(at, in_hbm(green0), *after)


def halo_kernel(moms, local, which_ref, *refs):
    pieces, out = refs[: 2 * moms], refs[-1]
    for dh in range(2):

        @pl.when(which_ref[0] == dh)
        def _(dh=dh):
            for dm in range(moms):
                out[dm * local : (dm + 1) * local] = pieces[dh * moms + dm][...]


def halo_call(place, odd, pieces, after):
    local, rows, orbitals = pieces[0].shape
    _, z, h, _ = place.here()
    which = (place.goes_up(z, odd) != (h == 1)).astype(jnp.int32).reshape(1)
    return pl.pallas_call(
        functools.partial(halo_kernel, place.moms, local),
        out_shape=jax.ShapeDtypeStruct((place.moms * local, rows, orbitals), jnp.bfloat16),
        in_specs=[pl.BlockSpec(memory_space=pltpu.SMEM)] + [in_vmem()] * len(pieces) + anywhere(after),
        out_specs=in_vmem(),
        compiler_params=pltpu.CompilerParams(vmem_limit_bytes=SMALL_VMEM),
        cost_estimate=pl.CostEstimate(flops=0, bytes_accessed=0, transcendentals=0),
        name="halo",
    )(which, *pieces, *after)


def smooth_kernel(n_in, n_add, splits, mix_ref, *refs):
    inputs, addends, outs = refs[:n_in], refs[n_in : n_in + n_add], refs[-len(splits) :]
    size, width = inputs[0].shape[-2:]
    for at in range(0, size, TILE):
        rows = slice(at, at + TILE)
        stacked = jnp.concatenate([r[:, rows].reshape(-1, width) for r in inputs], axis=0)
        mixed = jnp.dot(mix_ref[...], stacked, preferred_element_type=jnp.float32)
        for r in addends:
            mixed += r[:, rows].reshape(-1, width).astype(jnp.float32)
        mixed = mixed.astype(jnp.bfloat16).reshape(-1, TILE, width)
        for out, (first, last) in zip(outs, splits, strict=True):
            out[:, rows] = mixed[first:last]


def smooth_call(part, mix, inputs, addends, splits, after):
    size, orbitals = inputs[0].shape[1:]
    counts = [last - first for first, last in splits]
    return pl.pallas_call(
        functools.partial(smooth_kernel, len(inputs), len(addends), splits),
        out_shape=[jax.ShapeDtypeStruct((count, size, orbitals), jnp.bfloat16) for count in counts],
        in_specs=[in_vmem()] * (1 + len(inputs) + len(addends)) + anywhere(after),
        out_specs=[in_vmem()] * len(counts),
        compiler_params=pltpu.CompilerParams(vmem_limit_bytes=SMALL_VMEM),
        cost_estimate=pl.CostEstimate(flops=0, bytes_accessed=0, transcendentals=0),
        name="smooth",
    )(mix, *inputs, *addends, *after)


def dyson_kernel(pieces, row_ref, green_ref, phonon_ref, *refs):
    out_ref, energy, left, series = refs[-4:]
    size = phonon_ref.shape[0]
    low, high = slice(0, size), slice(size, 2 * size)

    def as_left(re, im):
        left[low, low] = re
        left[high, high] = re
        left[low, high] = -im
        left[high, low] = im

    for k, rows in enumerate(pieces):
        at = pl.multiple_of(row_ref[k], STEP)
        scale = phonon_ref[pl.ds(pl.multiple_of(row_ref[len(pieces) + k], STEP), rows), :].astype(jnp.float32)
        value = refs[k][0].astype(jnp.float32)
        energy[pl.ds(at, rows), :] = (scale * value).astype(jnp.bfloat16)
    as_left(green_ref[0, 0, 0], green_ref[0, 0, 1])
    product = jnp.dot(left[...], energy[...], preferred_element_type=jnp.float32)
    product = (product * (1.0 / size)).astype(jnp.bfloat16)
    as_left(product[low], product[high])
    green = green_ref[0, 0].reshape(2 * size, size)
    last = green
    for step in range(NEUMANN):
        added = green.astype(jnp.float32) + jnp.dot(left[...], last, preferred_element_type=jnp.float32)
        if step < NEUMANN - 1:
            series[...] = added.astype(jnp.bfloat16)
            last = series[...]
        else:
            out_ref[0, 0] = added.astype(jnp.bfloat16).reshape(2, size, size)


def dyson_call(place, green0, phonon_me, pieces, first, last, out):
    size = green0.shape[-1]
    m, z, h, q = place.here()
    at = jnp.stack([place.row(*place.source(m, h, shift), part) for part, shift, _, _ in pieces]).astype(jnp.int32)
    block = pl.BlockSpec((1, 1, 2, size, size), lambda e, t: (0, first + e, 0, 0, 0))
    specs = [block, pl.BlockSpec((size, size), lambda e, t: (0, 0))]
    for part, _, _, whole in pieces:
        start = first if whole else 0
        specs.append(pl.BlockSpec((1, part[1], size), lambda e, t, start=start: (start + e, 0, 0)))
    args = [jnp.concatenate([at, at % size]), in_hbm(green0), phonon_me] + [x for _, _, x, _ in pieces]
    aliases = {}
    if out is not None:
        aliases = {len(args): 0}
        args.append(out)
        specs.append(pl.BlockSpec(memory_space=pl.ANY))
    count = last - first
    return pl.pallas_call(
        functools.partial(dyson_kernel, [part[1] for part, _, _, _ in pieces]),
        out_shape=jax.ShapeDtypeStruct(green0.shape, green0.dtype),
        grid_spec=pltpu.PrefetchScalarGridSpec(
            num_scalar_prefetch=1,
            grid=(count,),
            in_specs=specs,
            out_specs=block,
            scratch_shapes=[
                pltpu.VMEM((2 * size, size), jnp.bfloat16),
                pltpu.VMEM((2 * size, 2 * size), jnp.bfloat16),
                pltpu.VMEM((2 * size, size), jnp.bfloat16),
            ],
        ),
        input_output_aliases=aliases,
        compiler_params=pltpu.CompilerParams(vmem_limit_bytes=VMEM_LIMIT),
        cost_estimate=pl.CostEstimate(flops=0, bytes_accessed=0, transcendentals=0),
        name="dyson",
    )(*args)


def per_device(green0, phonon_me, coupling, shift_table, offsets):
    local, orbitals = green0.shape[1], green0.shape[3]
    place = Place(local, orbitals)
    m, z, h, q = place.here()
    flat = green0.reshape(1, local, 2 * orbitals, orbitals)
    groups = ((0, local // 2), (local // 2, local))
    stay = place.shifts[0]
    last_made = []

    def cut_and_send(part):
        mine = cut_call(place, part, flat, last_made)
        last_made[:] = [mine[0]]
        return [
            piece if shift == stay else lax.ppermute(piece, AXES, place.shift_perm(shift))
            for shift, piece in zip(place.shifts, mine, strict=True)
        ]

    def send_halos(mine):
        halos = []
        for odd in range(2):
            halo = halo_call(place, odd, mine, last_made)
            last_made[:] = [halo]
            halos.append(lax.ppermute(halo, AXES, place.plane_perm(odd)))
        return list(mine) + halos

    count = len(place.shifts) * local
    back = [[] for _ in groups]

    def partial_sums(part, inputs):
        addends = []
        for dq in range(1, place.reach):
            (sums,) = smooth_call(part, mix[dq], inputs, [], [(0, count)], last_made)
            last_made[:] = [sums]
            addends.append(lax.ppermute(sums, AXES, place.swap_perm(dq)))
        return addends

    def send_back(part, inputs, addends):
        apart = part == place.parts[-1]
        cut = groups if apart else ((0, local),)
        splits = [(i * local + first, i * local + last) for first, last in cut for i in range(len(place.shifts))]
        mixed = smooth_call(part, mix[0], inputs, addends, splits, last_made)
        last_made[:] = [mixed[0]]
        for s in range(len(cut)):
            for i, shift in enumerate(place.shifts):
                piece = mixed[s * len(place.shifts) + i]
                if shift != stay:
                    piece = lax.ppermute(piece, AXES, place.shift_perm(shift))
                for g in range(len(groups)):
                    if g == s or not apart:
                        back[g].append((part, shift, piece, not apart))
        return [back[0][k - len(place.shifts)][2] for k in range(1, len(place.shifts))]

    parts = place.parts
    pieces = [cut_and_send(part) for part in parts]
    mix = mixing(place, coupling, shift_table, offsets, last_made)
    last_made[:] = [mix[0]]
    inputs = [send_halos(mine) for mine in pieces]
    sent = []
    for part, mine in zip(parts, inputs, strict=True):
        last_made += sent
        addends = partial_sums(part, mine)
        sent = send_back(part, mine, addends)
    out = None
    for (first, last), arrived in zip(groups, back, strict=True):
        out = dyson_call(place, green0, phonon_me, arrived, first, last, out)
    return out


def solution(mesh):
    in_specs = (P("mom", "en", None, None, None), P(), P(), P(), P())
    out_specs = P("mom", "en", None, None, None)
    return jax.shard_map(
        per_device, mesh=mesh, in_specs=in_specs, out_specs=out_specs, check_vma=False
    )
```

```python
import functools

import jax
import jax.numpy as jnp
from jax import lax
from jax.experimental import pallas as pl
from jax.experimental.pallas import tpu as pltpu
from jax.sharding import PartitionSpec as P

NEUMANN = 3
TILE = 16
STEP = 32
CUTS = 2
AXES = ("mom", "en")
HALO = 6_000_000_000
GATE = 60_000_000_000
SMALL_VMEM = 12 * 1024 * 1024
VMEM_LIMIT = 20 * 1024 * 1024
WIDTH = 256


class Place:
    def __init__(self, local_energies, orbitals):
        self.moms = lax.axis_size("mom")
        self.ens = lax.axis_size("en")
        self.local = local_energies
        self.energies = local_energies * self.ens
        self.reach = -(-(self.energies // 8) // local_energies)
        self.planes = self.ens // (2 * self.reach)
        assert self.planes * 2 * self.reach == self.ens
        self.block = 2 * orbitals // (2 * self.moms)
        units = self.block // STEP
        assert units * STEP == self.block
        sizes = [STEP * (units // CUTS + (i < units % CUTS)) for i in range(CUTS)]
        self.parts = [(sum(sizes[:i]), size) for i, size in enumerate(sizes) if size]
        self.shifts = [(dm, dh) for dh in range(2) for dm in range(self.moms)]

    def here(self):
        n = lax.axis_index("en")
        plane = 2 * self.reach
        return lax.axis_index("mom"), n // plane, (n // self.reach) % 2, n % self.reach

    def index(self, m, z, h, q):
        return m * self.ens + (z * 2 + h) * self.reach + q

    def everyone(self):
        return [
            (m, z, h, q)
            for m in range(self.moms)
            for z in range(self.planes)
            for h in range(2)
            for q in range(self.reach)
        ]

    def target(self, m, h, shift):
        return (m + shift[0]) % self.moms, (h + shift[1]) % 2

    def source(self, m, h, shift):
        return (m - shift[0]) % self.moms, (h + shift[1]) % 2

    def row(self, m, h, part):
        return (m * 2 + h) * self.block + part[0]

    def shift_perm(self, shift):
        pairs = []
        for m, z, h, q in self.everyone():
            tm, th = self.target(m, h, shift)
            pairs.append((self.index(m, z, h, q), self.index(tm, z, th, q)))
        return pairs

    def goes_up(self, z, odd):
        return z % 2 == odd

    def plane_perm(self, odd):
        pairs = []
        for m, z, h, q in self.everyone():
            to = z + 1 if self.goes_up(z, odd) else z - 1
            if 0 <= to < self.planes:
                pairs.append((self.index(m, z, h, q), self.index(m, to, h, q)))
        return pairs

    def swap_perm(self, dq):
        return [
            (self.index(m, z, h, q), self.index(m, z, h, (q + dq) % self.reach))
            for m, z, h, q in self.everyone()
        ]

    def first_energy(self, z, h, q):
        return ((z * 2 + h) * self.reach + q) * self.local


def mix_kernel(place, coupling_ref, shift_ref, offset_ref, here_ref, *outs):
    m, z, h, q = here_ref[0], here_ref[1], here_ref[2], here_ref[3]
    count = len(place.shifts) * place.local
    shape = (place.reach * count, 2 * count)
    row = lax.broadcasted_iota(jnp.int32, shape, 0)
    column = lax.broadcasted_iota(jnp.int32, shape, 1)

    def energy(plane, half, at, of):
        return ((plane * 2 + half) * place.reach + at) * place.local + of % place.local

    shift = (row // place.local) % len(place.shifts)
    target_mom = (m + shift % place.moms) % place.moms
    target_energy = energy(z, (h + shift // place.moms) % 2, (q + row // count) % place.reach, row)
    shift = (column // place.local) % len(place.shifts)
    second = shift // place.moms
    up = (z + second) % 2 == 0
    near = column < count
    plane = jnp.where(near, z, jnp.where(up, z + 1, z - 1))
    half = jnp.where(near, (h + second) % 2, jnp.where(up, 0, 1))
    source_mom = (m + place.moms - shift % place.moms) % place.moms
    source_energy = energy(plane, half, q, column)
    real = (source_energy >= 0) & (source_energy < place.energies)
    apart = jnp.where(real, target_energy - source_energy, 2 * place.energies)
    table = jnp.zeros(shape, jnp.float32)
    for k in range(place.moms):
        here = target_mom == k
        for w in range(offset_ref.shape[0]):
            chosen = here & (source_mom == shift_ref[k, w])
            table += jnp.where(chosen & (apart == offset_ref[w]), coupling_ref[0, k, w], 0.0)
            table += jnp.where(chosen & (apart == -offset_ref[w]), coupling_ref[1, k, w], 0.0)
    table = table.astype(jnp.bfloat16)
    wide = (2 * count, 2 * count * TILE)
    spread = (
        lax.broadcasted_iota(jnp.int32, wide, 0) == lax.broadcasted_iota(jnp.int32, wide, 1) // TILE
    ).astype(jnp.bfloat16)
    tall = (count * TILE, count)
    repeat = (
        lax.broadcasted_iota(jnp.int32, tall, 0) // TILE == lax.broadcasted_iota(jnp.int32, tall, 1)
    ).astype(jnp.bfloat16)
    full = (count * TILE, 2 * count * TILE)
    diagonal = lax.broadcasted_iota(jnp.int32, full, 0) % TILE == lax.broadcasted_iota(jnp.int32, full, 1) % TILE
    for dq, out in enumerate(outs):
        part = table[dq * count : (dq + 1) * count]
        part = jnp.dot(part, spread, preferred_element_type=jnp.float32).astype(jnp.bfloat16)
        part = jnp.dot(repeat, part, preferred_element_type=jnp.float32)
        out[...] = jnp.where(diagonal, part, 0.0).astype(jnp.bfloat16)


def mixing(place, coupling, shift_table, offsets, after):
    count = len(place.shifts) * place.local
    shape = (count * TILE, 2 * count * TILE)
    smem = pl.BlockSpec(memory_space=pltpu.SMEM)

    def kernel(coupling_ref, shift_ref, offset_ref, here_ref, *refs):
        mix_kernel(place, coupling_ref, shift_ref, offset_ref, here_ref, *refs[len(after) :])

    return pl.pallas_call(
        kernel,
        out_shape=[jax.ShapeDtypeStruct(shape, jnp.bfloat16)] * place.reach,
        in_specs=[smem] * 4 + anywhere(after),
        out_specs=[in_vmem()] * place.reach,
        compiler_params=pltpu.CompilerParams(vmem_limit_bytes=2 * SMALL_VMEM),
        cost_estimate=pl.CostEstimate(flops=0, bytes_accessed=0, transcendentals=0),
        name="mixing",
    )(coupling, shift_table, offsets, jnp.stack(place.here()).astype(jnp.int32), *after)


def in_vmem():
    return pl.BlockSpec(memory_space=pltpu.VMEM)


def in_hbm(x):
    return pltpu.with_memory_space_constraint(x, pltpu.HBM)


def anywhere(arrays):
    return [pl.BlockSpec(memory_space=pl.ANY)] * len(arrays)


def cut_kernel(n, sizes, at_ref, green_ref, *refs):
    outs, sems = refs[-n - 1 : -1], refs[-1]
    copies = []
    for k, out in enumerate(outs):
        rows = pl.ds(pl.multiple_of(at_ref[k], STEP), sizes)
        copies.append(pltpu.make_async_copy(green_ref.at[0, :, rows, :], out, sems.at[k]))
    for copy in copies:
        copy.start()
    for copy in copies:
        copy.wait()


def cut_call(place, part, green0, after):
    local, orbitals = place.local, green0.shape[-1]
    m, z, h, q = place.here()
    at = jnp.stack([place.row(*place.target(m, h, shift), part) for shift in place.shifts]).astype(jnp.int32)
    shape = (local, part[1], orbitals)
    n = len(place.shifts)
    return pl.pallas_call(
        functools.partial(cut_kernel, n, part[1]),
        out_shape=[jax.ShapeDtypeStruct(shape, jnp.bfloat16)] * n,
        in_specs=[pl.BlockSpec(memory_space=pltpu.SMEM)] + anywhere([green0, *after]),
        out_specs=[in_vmem()] * n,
        scratch_shapes=[pltpu.SemaphoreType.DMA((n,))],
        compiler_params=pltpu.CompilerParams(vmem_limit_bytes=SMALL_VMEM),
        cost_estimate=pl.CostEstimate(flops=0, bytes_accessed=0, transcendentals=0),
        name="cut",
    )(at, in_hbm(green0), *after)


def halo_kernel(moms, local, which_ref, *refs):
    pieces, outs, sems = refs[: 2 * moms], refs[-3:-1], refs[-1]
    for first in range(2):

        @pl.when(which_ref[0] == first)
        def _(first=first):
            copies = []
            for dh, out in zip((first, 1 - first), outs, strict=True):
                for dm in range(moms):
                    k = dh * moms + dm
                    rows = out.at[pl.ds(dm * local, local)]
                    copies.append(pltpu.make_async_copy(pieces[k], rows, sems.at[k]))
            for copy in copies:
                copy.start()
            for copy in copies:
                copy.wait()


def halo_call(place, pieces, after):
    local, rows, orbitals = pieces[0].shape
    _, z, h, _ = place.here()
    which = (place.goes_up(z, 0) != (h == 1)).astype(jnp.int32).reshape(1)
    return pl.pallas_call(
        functools.partial(halo_kernel, place.moms, local),
        out_shape=[jax.ShapeDtypeStruct((place.moms * local, rows, orbitals), jnp.bfloat16)] * 2,
        in_specs=[pl.BlockSpec(memory_space=pltpu.SMEM)] + anywhere([*pieces, *after]),
        out_specs=[in_vmem()] * 2,
        scratch_shapes=[pltpu.SemaphoreType.DMA((len(pieces),))],
        compiler_params=pltpu.CompilerParams(vmem_limit_bytes=SMALL_VMEM),
        cost_estimate=pl.CostEstimate(flops=0, bytes_accessed=0, transcendentals=0),
        name="halo",
    )(which, *pieces, *after)


def gate_kernel(*refs):
    refs[-1][...] = jnp.zeros_like(refs[-1])


def gate_call(weight, after):
    return pl.pallas_call(
        gate_kernel,
        out_shape=jax.ShapeDtypeStruct((8, 128), jnp.float32),
        in_specs=anywhere(after),
        out_specs=in_vmem(),
        compiler_params=pltpu.CompilerParams(vmem_limit_bytes=SMALL_VMEM),
        cost_estimate=pl.CostEstimate(flops=weight, bytes_accessed=0, transcendentals=0),
        name="gate",
    )(*after)


def smooth_kernel(n_in, n_add, n_out, mix_ref, *refs):
    inputs, addends, outs = refs[:n_in], refs[n_in : n_in + n_add], refs[-n_out:]
    size, width = inputs[0].shape[-2:]
    for at in range(0, size, TILE):
        rows = slice(at, at + TILE)
        stacked = jnp.concatenate([r[:, rows].reshape(-1, width) for r in inputs], axis=0)
        mixed = jnp.dot(mix_ref[...], stacked, preferred_element_type=jnp.float32)
        for r in addends:
            mixed += r[:, rows].reshape(-1, width).astype(jnp.float32)
        mixed = mixed.astype(jnp.bfloat16).reshape(-1, TILE, width)
        count = mixed.shape[0] // n_out
        for k, out in enumerate(outs):
            out[:, rows] = mixed[k * count : (k + 1) * count]


def smooth_call(mix, inputs, addends, outs, after):
    size, orbitals = inputs[0].shape[1:]
    count = mix.shape[0] // TILE // outs
    return pl.pallas_call(
        functools.partial(smooth_kernel, len(inputs), len(addends), outs),
        out_shape=[jax.ShapeDtypeStruct((count, size, orbitals), jnp.bfloat16)] * outs,
        in_specs=[in_vmem()] * (1 + len(inputs) + len(addends)) + anywhere(after),
        out_specs=[in_vmem()] * outs,
        compiler_params=pltpu.CompilerParams(vmem_limit_bytes=SMALL_VMEM),
        cost_estimate=pl.CostEstimate(flops=0, bytes_accessed=0, transcendentals=0),
        name="smooth",
    )(mix, *inputs, *addends, *after)


def part_kernel(local, group, sums_ref, *refs):
    outs, sems = refs[-1 - sums_ref.shape[0] // local : -1], refs[-1]
    first, last = group
    copies = [
        pltpu.make_async_copy(sums_ref.at[pl.ds(k * local + first, last - first)], out, sems.at[k])
        for k, out in enumerate(outs)
    ]
    for copy in copies:
        copy.start()
    for copy in copies:
        copy.wait()


def part_call(place, sums, group, after):
    slots = len(place.shifts)
    return pl.pallas_call(
        functools.partial(part_kernel, place.local, group),
        out_shape=[pltpu.HBM((group[1] - group[0],) + sums.shape[1:], jnp.bfloat16)] * slots,
        in_specs=[in_vmem()] + anywhere(after),
        out_specs=anywhere(place.shifts),
        scratch_shapes=[pltpu.SemaphoreType.DMA((slots,))],
        compiler_params=pltpu.CompilerParams(vmem_limit_bytes=SMALL_VMEM),
        cost_estimate=pl.CostEstimate(flops=0, bytes_accessed=0, transcendentals=0),
        name="part",
    )(sums, *after)


def dyson_kernel(pieces, row_ref, green_ref, phonon_ref, *refs):
    out_ref, left, even, odd = refs[-4:]
    size = phonon_ref.shape[0]
    for k, rows in enumerate(pieces):
        at = pl.multiple_of(row_ref[k], STEP)
        scale = phonon_ref[pl.ds(at, rows), :].astype(jnp.float32)
        value = refs[k][0].astype(jnp.float32)
        odd[row_ref[len(pieces) + k], pl.ds(at, rows), :] = (scale * value).astype(jnp.bfloat16)
    odd[2] = odd[0] + odd[1]

    def hold(to, ref):
        to[0] = ref[0, 0, 0]
        to[1] = ref[0, 0, 1]
        to[2] = ref[0, 0, 0] + ref[0, 0, 1]

    def product(right, put):
        for at in range(0, size, WIDTH):
            columns = slice(at, at + WIDTH)
            p, q, t = (
                jnp.dot(left[c], right[c, :, columns], preferred_element_type=jnp.float32) for c in range(3)
            )
            put(columns, p - q, t - (p + q))

    def put_transfer(columns, re, im):
        out_ref[0, 0, 0, :, columns] = (re * (1.0 / size)).astype(jnp.bfloat16)
        out_ref[0, 0, 1, :, columns] = (im * (1.0 / size)).astype(jnp.bfloat16)

    hold(left, green_ref)
    hold(even, green_ref)
    product(odd, put_transfer)
    hold(left, out_ref)
    for step in range(NEUMANN):
        right, to = (even, odd) if step % 2 == 0 else (odd, even)

        def put(columns, re, im, to=to, final=step == NEUMANN - 1):
            re = (re + green_ref[0, 0, 0, :, columns].astype(jnp.float32)).astype(jnp.bfloat16)
            im = (im + green_ref[0, 0, 1, :, columns].astype(jnp.float32)).astype(jnp.bfloat16)
            if final:
                out_ref[0, 0, 0, :, columns] = re
                out_ref[0, 0, 1, :, columns] = im
            else:
                to[0, :, columns] = re
                to[1, :, columns] = im
                to[2, :, columns] = re + im

        product(right, put)


def dyson_call(place, green0, phonon_me, pieces, first, last, out):
    size = green0.shape[-1]
    m, z, h, q = place.here()
    at = jnp.stack([place.row(*place.source(m, h, shift), part) for part, shift, _, _ in pieces]).astype(jnp.int32)
    block = pl.BlockSpec((1, 1, 2, size, size), lambda e, t: (0, first + e, 0, 0, 0))
    specs = [block, pl.BlockSpec((size, size), lambda e, t: (0, 0))]
    for part, _, _, whole in pieces:
        start = first if whole else 0
        specs.append(pl.BlockSpec((1, part[1], size), lambda e, t, start=start: (start + e, 0, 0)))
    args = [jnp.concatenate([at % size, at // size]), in_hbm(green0), phonon_me] + [x for _, _, x, _ in pieces]
    aliases = {}
    if out is not None:
        aliases = {len(args): 0}
        args.append(out)
        specs.append(pl.BlockSpec(memory_space=pl.ANY))
    count = last - first
    return pl.pallas_call(
        functools.partial(dyson_kernel, [part[1] for part, _, _, _ in pieces]),
        out_shape=jax.ShapeDtypeStruct(green0.shape, green0.dtype),
        grid_spec=pltpu.PrefetchScalarGridSpec(
            num_scalar_prefetch=1,
            grid=(count,),
            in_specs=specs,
            out_specs=block,
            scratch_shapes=[pltpu.VMEM((3, size, size), jnp.bfloat16)] * 3,
        ),
        input_output_aliases=aliases,
        compiler_params=pltpu.CompilerParams(vmem_limit_bytes=VMEM_LIMIT),
        cost_estimate=pl.CostEstimate(
            flops=count * (NEUMANN + 1) * 8 * size**3, bytes_accessed=(6 * count + 1) * 2 * size * size, transcendentals=0
        ),
        name="dyson",
    )(*args)


def per_device(green0, phonon_me, coupling, shift_table, offsets):
    local, orbitals = green0.shape[1], green0.shape[3]
    place = Place(local, orbitals)
    m, z, h, q = place.here()
    flat = green0.reshape(1, local, 2 * orbitals, orbitals)
    groups = ((0, local // 2), (local // 2, local))
    stay = place.shifts[0]
    last_made = []

    def cut_and_send(part):
        mine = cut_call(place, part, flat, last_made)
        last_made[:] = [mine[0]]
        return [
            piece if shift == stay else lax.ppermute(piece, AXES, place.shift_perm(shift))
            for shift, piece in zip(place.shifts, mine, strict=True)
        ]

    def send_halos(mine):
        halos = halo_call(place, mine, last_made)
        last_made[:] = [halos[0]]
        return list(mine) + [lax.ppermute(x, AXES, place.plane_perm(odd)) for odd, x in enumerate(halos)]

    back = [[] for _ in groups]

    def partial_sums(inputs):
        addends = []
        for dq in range(1, place.reach):
            (sums,) = smooth_call(mix[dq], inputs, [], 1, last_made)
            last_made[:] = [sums]
            addends.append(lax.ppermute(sums, AXES, place.swap_perm(dq)))
        return addends

    def send_back(part, mixed, group):
        last_made[:] = [mixed[0]]
        arrived = []
        for shift, piece in zip(place.shifts, mixed, strict=True):
            if shift != stay:
                piece = lax.ppermute(piece, AXES, place.shift_perm(shift))
            arrived.append(piece)
            for g in range(len(groups)):
                if group in (g, None):
                    back[g].append((part, shift, piece, group is None))
        return arrived[1:]

    parts = place.parts
    pieces = [cut_and_send(part) for part in parts]
    mix = mixing(place, coupling, shift_table, offsets, last_made)
    last_made[:] = [mix[0]]
    inputs = [send_halos(mine) for mine in pieces]
    last_made[:] = [gate_call(HALO, last_made)]
    sent = []
    for part, mine in zip(parts, inputs, strict=True):
        addends = partial_sums(mine)
        if sent:
            last_made[:] = [gate_call(GATE, last_made + sent)]
        if part != parts[-1]:
            sent = send_back(part, smooth_call(mix[0], mine, addends, len(place.shifts), last_made), None)
            continue
        (sums,) = smooth_call(mix[0], mine, addends, 1, last_made)
        last_made[:] = [sums]
        for g, group in enumerate(groups):
            send_back(part, part_call(place, sums, group, last_made), g)
    out = None
    for (first, last), arrived in zip(groups, back, strict=True):
        out = dyson_call(place, green0, phonon_me, arrived, first, last, out)
    return out


def solution(mesh):
    in_specs = (P("mom", "en", None, None, None), P(), P(), P(), P())
    out_specs = P("mom", "en", None, None, None)
    return jax.shard_map(
        per_device, mesh=mesh, in_specs=in_specs, out_specs=out_specs, check_vma=False
    )
```

```python
import functools

import jax
import jax.numpy as jnp
from jax import lax
from jax.experimental import pallas as pl
from jax.experimental.pallas import tpu as pltpu
from jax.sharding import PartitionSpec as P

NEUMANN = 3
TILE = 16
STEP = 32
CUTS = 2
AXES = ("mom", "en")
HALO = 6_000_000_000
GATE = 60_000_000_000
SMALL_VMEM = 12 * 1024 * 1024
VMEM_LIMIT = 20 * 1024 * 1024
WIDTH = 256


class Place:
    def __init__(self, local_energies, orbitals):
        self.moms = lax.axis_size("mom")
        self.ens = lax.axis_size("en")
        self.local = local_energies
        self.energies = local_energies * self.ens
        self.reach = -(-(self.energies // 8) // local_energies)
        self.planes = self.ens // (2 * self.reach)
        assert self.planes * 2 * self.reach == self.ens
        self.block = 2 * orbitals // (2 * self.moms)
        units = self.block // STEP
        assert units * STEP == self.block
        sizes = [STEP * (units // CUTS + (i < units % CUTS)) for i in range(CUTS)]
        self.parts = [(sum(sizes[:i]), size) for i, size in enumerate(sizes) if size]
        self.shifts = [(dm, dh) for dh in range(2) for dm in range(self.moms)]

    def here(self):
        n = lax.axis_index("en")
        plane = 2 * self.reach
        return lax.axis_index("mom"), n // plane, (n // self.reach) % 2, n % self.reach

    def index(self, m, z, h, q):
        return m * self.ens + (z * 2 + h) * self.reach + q

    def everyone(self):
        return [
            (m, z, h, q)
            for m in range(self.moms)
            for z in range(self.planes)
            for h in range(2)
            for q in range(self.reach)
        ]

    def target(self, m, h, shift):
        return (m + shift[0]) % self.moms, (h + shift[1]) % 2

    def source(self, m, h, shift):
        return (m - shift[0]) % self.moms, (h + shift[1]) % 2

    def row(self, m, h, part):
        return (m * 2 + h) * self.block + part[0]

    def shift_perm(self, shift):
        pairs = []
        for m, z, h, q in self.everyone():
            tm, th = self.target(m, h, shift)
            pairs.append((self.index(m, z, h, q), self.index(tm, z, th, q)))
        return pairs

    def goes_up(self, z, odd):
        return z % 2 == odd

    def plane_perm(self, odd):
        pairs = []
        for m, z, h, q in self.everyone():
            to = z + 1 if self.goes_up(z, odd) else z - 1
            if 0 <= to < self.planes:
                pairs.append((self.index(m, z, h, q), self.index(m, to, h, q)))
        return pairs

    def swap_perm(self, dq):
        return [
            (self.index(m, z, h, q), self.index(m, z, h, (q + dq) % self.reach))
            for m, z, h, q in self.everyone()
        ]

    def first_energy(self, z, h, q):
        return ((z * 2 + h) * self.reach + q) * self.local


def mix_kernel(place, coupling_ref, shift_ref, offset_ref, here_ref, *outs):
    m, z, h, q = here_ref[0], here_ref[1], here_ref[2], here_ref[3]
    count = len(place.shifts) * place.local
    shape = (place.reach * count, 2 * count)
    row = lax.broadcasted_iota(jnp.int32, shape, 0)
    column = lax.broadcasted_iota(jnp.int32, shape, 1)

    def energy(plane, half, at, of):
        return ((plane * 2 + half) * place.reach + at) * place.local + of % place.local

    shift = (row // place.local) % len(place.shifts)
    target_mom = (m + shift % place.moms) % place.moms
    target_energy = energy(z, (h + shift // place.moms) % 2, (q + row // count) % place.reach, row)
    shift = (column // place.local) % len(place.shifts)
    second = shift // place.moms
    up = (z + second) % 2 == 0
    near = column < count
    plane = jnp.where(near, z, jnp.where(up, z + 1, z - 1))
    half = jnp.where(near, (h + second) % 2, jnp.where(up, 0, 1))
    source_mom = (m + place.moms - shift % place.moms) % place.moms
    source_energy = energy(plane, half, q, column)
    real = (source_energy >= 0) & (source_energy < place.energies)
    apart = jnp.where(real, target_energy - source_energy, 2 * place.energies)
    table = jnp.zeros(shape, jnp.float32)
    for k in range(place.moms):
        here = target_mom == k
        for w in range(offset_ref.shape[0]):
            chosen = here & (source_mom == shift_ref[k, w])
            table += jnp.where(chosen & (apart == offset_ref[w]), coupling_ref[0, k, w], 0.0)
            table += jnp.where(chosen & (apart == -offset_ref[w]), coupling_ref[1, k, w], 0.0)
    table = table.astype(jnp.bfloat16)
    wide = (2 * count, 2 * count * TILE)
    spread = (
        lax.broadcasted_iota(jnp.int32, wide, 0) == lax.broadcasted_iota(jnp.int32, wide, 1) // TILE
    ).astype(jnp.bfloat16)
    tall = (count * TILE, count)
    repeat = (
        lax.broadcasted_iota(jnp.int32, tall, 0) // TILE == lax.broadcasted_iota(jnp.int32, tall, 1)
    ).astype(jnp.bfloat16)
    full = (count * TILE, 2 * count * TILE)
    diagonal = lax.broadcasted_iota(jnp.int32, full, 0) % TILE == lax.broadcasted_iota(jnp.int32, full, 1) % TILE
    for dq, out in enumerate(outs):
        part = table[dq * count : (dq + 1) * count]
        part = jnp.dot(part, spread, preferred_element_type=jnp.float32).astype(jnp.bfloat16)
        part = jnp.dot(repeat, part, preferred_element_type=jnp.float32)
        out[...] = jnp.where(diagonal, part, 0.0).astype(jnp.bfloat16)


def mixing(place, coupling, shift_table, offsets, after):
    count = len(place.shifts) * place.local
    shape = (count * TILE, 2 * count * TILE)
    smem = pl.BlockSpec(memory_space=pltpu.SMEM)

    def kernel(coupling_ref, shift_ref, offset_ref, here_ref, *refs):
        mix_kernel(place, coupling_ref, shift_ref, offset_ref, here_ref, *refs[len(after) :])

    return pl.pallas_call(
        kernel,
        out_shape=[jax.ShapeDtypeStruct(shape, jnp.bfloat16)] * place.reach,
        in_specs=[smem] * 4 + anywhere(after),
        out_specs=[in_vmem()] * place.reach,
        compiler_params=pltpu.CompilerParams(vmem_limit_bytes=2 * SMALL_VMEM),
        cost_estimate=pl.CostEstimate(flops=0, bytes_accessed=0, transcendentals=0),
        name="mixing",
    )(coupling, shift_table, offsets, jnp.stack(place.here()).astype(jnp.int32), *after)


def in_vmem():
    return pl.BlockSpec(memory_space=pltpu.VMEM)


def in_hbm(x):
    return pltpu.with_memory_space_constraint(x, pltpu.HBM)


def anywhere(arrays):
    return [pl.BlockSpec(memory_space=pl.ANY)] * len(arrays)


def cut_kernel(n, sizes, at_ref, green_ref, *refs):
    outs, sems = refs[-n - 1 : -1], refs[-1]
    copies = []
    for k, out in enumerate(outs):
        rows = pl.ds(pl.multiple_of(at_ref[k], STEP), sizes)
        copies.append(pltpu.make_async_copy(green_ref.at[0, :, rows, :], out, sems.at[k]))
    for copy in copies:
        copy.start()
    for copy in copies:
        copy.wait()


def cut_call(place, part, green0, after):
    local, orbitals = place.local, green0.shape[-1]
    m, z, h, q = place.here()
    at = jnp.stack([place.row(*place.target(m, h, shift), part) for shift in place.shifts]).astype(jnp.int32)
    shape = (local, part[1], orbitals)
    n = len(place.shifts)
    return pl.pallas_call(
        functools.partial(cut_kernel, n, part[1]),
        out_shape=[jax.ShapeDtypeStruct(shape, jnp.bfloat16)] * n,
        in_specs=[pl.BlockSpec(memory_space=pltpu.SMEM)] + anywhere([green0, *after]),
        out_specs=[in_vmem()] * n,
        scratch_shapes=[pltpu.SemaphoreType.DMA((n,))],
        compiler_params=pltpu.CompilerParams(vmem_limit_bytes=SMALL_VMEM),
        cost_estimate=pl.CostEstimate(flops=0, bytes_accessed=0, transcendentals=0),
        name="cut",
    )(at, in_hbm(green0), *after)


def halo_kernel(moms, local, which_ref, *refs):
    pieces, outs, sems = refs[: 2 * moms], refs[-3:-1], refs[-1]
    for first in range(2):

        @pl.when(which_ref[0] == first)
        def _(first=first):
            copies = []
            for dh, out in zip((first, 1 - first), outs, strict=True):
                for dm in range(moms):
                    k = dh * moms + dm
                    rows = out.at[pl.ds(dm * local, local)]
                    copies.append(pltpu.make_async_copy(pieces[k], rows, sems.at[k]))
            for copy in copies:
                copy.start()
            for copy in copies:
                copy.wait()


def halo_call(place, pieces, after):
    local, rows, orbitals = pieces[0].shape
    _, z, h, _ = place.here()
    which = (place.goes_up(z, 0) != (h == 1)).astype(jnp.int32).reshape(1)
    return pl.pallas_call(
        functools.partial(halo_kernel, place.moms, local),
        out_shape=[jax.ShapeDtypeStruct((place.moms * local, rows, orbitals), jnp.bfloat16)] * 2,
        in_specs=[pl.BlockSpec(memory_space=pltpu.SMEM)] + anywhere([*pieces, *after]),
        out_specs=[in_vmem()] * 2,
        scratch_shapes=[pltpu.SemaphoreType.DMA((len(pieces),))],
        compiler_params=pltpu.CompilerParams(vmem_limit_bytes=SMALL_VMEM),
        cost_estimate=pl.CostEstimate(flops=0, bytes_accessed=0, transcendentals=0),
        name="halo",
    )(which, *pieces, *after)


def gate_kernel(*refs):
    refs[-1][...] = jnp.zeros_like(refs[-1])


def gate_call(weight, after):
    return pl.pallas_call(
        gate_kernel,
        out_shape=jax.ShapeDtypeStruct((8, 128), jnp.float32),
        in_specs=anywhere(after),
        out_specs=in_vmem(),
        compiler_params=pltpu.CompilerParams(vmem_limit_bytes=SMALL_VMEM),
        cost_estimate=pl.CostEstimate(flops=weight, bytes_accessed=0, transcendentals=0),
        name="gate",
    )(*after)


def smooth_kernel(n_in, n_add, n_out, mix_ref, *refs):
    inputs, addends, outs = refs[:n_in], refs[n_in : n_in + n_add], refs[-n_out:]
    size, width = inputs[0].shape[-2:]
    for at in range(0, size, TILE):
        rows = slice(at, at + TILE)
        stacked = jnp.concatenate([r[:, rows].reshape(-1, width) for r in inputs], axis=0)
        mixed = jnp.dot(mix_ref[...], stacked, preferred_element_type=jnp.float32)
        for r in addends:
            mixed += r[:, rows].reshape(-1, width).astype(jnp.float32)
        mixed = mixed.astype(jnp.bfloat16).reshape(-1, TILE, width)
        count = mixed.shape[0] // n_out
        for k, out in enumerate(outs):
            out[:, rows] = mixed[k * count : (k + 1) * count]


def smooth_call(mix, inputs, addends, outs, after):
    size, orbitals = inputs[0].shape[1:]
    count = mix.shape[0] // TILE // outs
    return pl.pallas_call(
        functools.partial(smooth_kernel, len(inputs), len(addends), outs),
        out_shape=[jax.ShapeDtypeStruct((count, size, orbitals), jnp.bfloat16)] * outs,
        in_specs=[in_vmem()] * (1 + len(inputs) + len(addends)) + anywhere(after),
        out_specs=[in_vmem()] * outs,
        compiler_params=pltpu.CompilerParams(vmem_limit_bytes=SMALL_VMEM),
        cost_estimate=pl.CostEstimate(flops=0, bytes_accessed=0, transcendentals=0),
        name="smooth",
    )(mix, *inputs, *addends, *after)


def add_kernel(n_add, slots, lead, *refs):
    terms, local = refs[: 1 + n_add], refs[0].shape[0] // slots
    outs, rest = refs[-slots:], refs[-1 - slots]
    for k in range(slots):
        energies = slice(k * local, (k + 1) * local)
        total = sum(r[energies].astype(jnp.float32) for r in terms).astype(jnp.bfloat16)
        outs[k][...] = total[:lead]
        if lead < local:
            rest[k * (local - lead) : (k + 1) * (local - lead)] = total[lead:]


def add_call(place, terms, lead, after):
    slots, tail = len(place.shifts), terms[0].shape[1:]
    counts = [slots * (place.local - lead)] * (lead < place.local) + [lead] * slots
    return pl.pallas_call(
        functools.partial(add_kernel, len(terms) - 1, slots, lead),
        out_shape=[jax.ShapeDtypeStruct((count,) + tail, jnp.bfloat16) for count in counts],
        in_specs=[in_vmem()] * len(terms) + anywhere(after),
        out_specs=[in_vmem()] * len(counts),
        compiler_params=pltpu.CompilerParams(vmem_limit_bytes=SMALL_VMEM),
        cost_estimate=pl.CostEstimate(flops=0, bytes_accessed=0, transcendentals=0),
        name="add",
    )(*terms, *after)


def part_kernel(count, sums_ref, *refs):
    outs, sems = refs[-1 - sums_ref.shape[0] // count : -1], refs[-1]
    copies = [
        pltpu.make_async_copy(sums_ref.at[pl.ds(k * count, count)], out, sems.at[k]) for k, out in enumerate(outs)
    ]
    for copy in copies:
        copy.start()
    for copy in copies:
        copy.wait()


def part_call(place, sums, after):
    slots = len(place.shifts)
    count = sums.shape[0] // slots
    return pl.pallas_call(
        functools.partial(part_kernel, count),
        out_shape=[pltpu.HBM((count,) + sums.shape[1:], jnp.bfloat16)] * slots,
        in_specs=[in_vmem()] + anywhere(after),
        out_specs=anywhere(place.shifts),
        scratch_shapes=[pltpu.SemaphoreType.DMA((slots,))],
        compiler_params=pltpu.CompilerParams(vmem_limit_bytes=SMALL_VMEM),
        cost_estimate=pl.CostEstimate(flops=0, bytes_accessed=0, transcendentals=0),
        name="part",
    )(sums, *after)


def dyson_kernel(pieces, row_ref, green_ref, phonon_ref, *refs):
    out_ref, left, even, odd = refs[-4:]
    size = phonon_ref.shape[0]
    for k, rows in enumerate(pieces):
        at = pl.multiple_of(row_ref[k], STEP)
        scale = phonon_ref[pl.ds(at, rows), :].astype(jnp.float32)
        value = refs[k][0].astype(jnp.float32)
        odd[row_ref[len(pieces) + k], pl.ds(at, rows), :] = (scale * value).astype(jnp.bfloat16)
    odd[2] = odd[0] + odd[1]

    def hold(to, ref):
        to[0] = ref[0, 0, 0]
        to[1] = ref[0, 0, 1]
        to[2] = ref[0, 0, 0] + ref[0, 0, 1]

    def product(right, put):
        for at in range(0, size, WIDTH):
            columns = slice(at, at + WIDTH)
            p, q, t = (
                jnp.dot(left[c], right[c, :, columns], preferred_element_type=jnp.float32) for c in range(3)
            )
            put(columns, p - q, t - (p + q))

    def put_transfer(columns, re, im):
        out_ref[0, 0, 0, :, columns] = (re * (1.0 / size)).astype(jnp.bfloat16)
        out_ref[0, 0, 1, :, columns] = (im * (1.0 / size)).astype(jnp.bfloat16)

    hold(left, green_ref)
    hold(even, green_ref)
    product(odd, put_transfer)
    hold(left, out_ref)
    for step in range(NEUMANN):
        right, to = (even, odd) if step % 2 == 0 else (odd, even)

        def put(columns, re, im, to=to, final=step == NEUMANN - 1):
            re = (re + green_ref[0, 0, 0, :, columns].astype(jnp.float32)).astype(jnp.bfloat16)
            im = (im + green_ref[0, 0, 1, :, columns].astype(jnp.float32)).astype(jnp.bfloat16)
            if final:
                out_ref[0, 0, 0, :, columns] = re
                out_ref[0, 0, 1, :, columns] = im
            else:
                to[0, :, columns] = re
                to[1, :, columns] = im
                to[2, :, columns] = re + im

        product(right, put)


def dyson_call(place, green0, phonon_me, pieces, first, last, out):
    size = green0.shape[-1]
    m, z, h, q = place.here()
    at = jnp.stack([place.row(*place.source(m, h, shift), part) for part, shift, _, _ in pieces]).astype(jnp.int32)
    block = pl.BlockSpec((1, 1, 2, size, size), lambda e, t: (0, first + e, 0, 0, 0))
    specs = [block, pl.BlockSpec((size, size), lambda e, t: (0, 0))]
    for part, _, _, whole in pieces:
        start = first if whole else 0
        specs.append(pl.BlockSpec((1, part[1], size), lambda e, t, start=start: (start + e, 0, 0)))
    args = [jnp.concatenate([at % size, at // size]), in_hbm(green0), phonon_me] + [x for _, _, x, _ in pieces]
    aliases = {}
    if out is not None:
        aliases = {len(args): 0}
        args.append(out)
        specs.append(pl.BlockSpec(memory_space=pl.ANY))
    count = last - first
    return pl.pallas_call(
        functools.partial(dyson_kernel, [part[1] for part, _, _, _ in pieces]),
        out_shape=jax.ShapeDtypeStruct(green0.shape, green0.dtype),
        grid_spec=pltpu.PrefetchScalarGridSpec(
            num_scalar_prefetch=1,
            grid=(count,),
            in_specs=specs,
            out_specs=block,
            scratch_shapes=[pltpu.VMEM((3, size, size), jnp.bfloat16)] * 3,
        ),
        input_output_aliases=aliases,
        compiler_params=pltpu.CompilerParams(vmem_limit_bytes=VMEM_LIMIT),
        cost_estimate=pl.CostEstimate(
            flops=count * (NEUMANN + 1) * 8 * size**3, bytes_accessed=(6 * count + 1) * 2 * size * size, transcendentals=0
        ),
        name="dyson",
    )(*args)


def per_device(green0, phonon_me, coupling, shift_table, offsets):
    local, orbitals = green0.shape[1], green0.shape[3]
    place = Place(local, orbitals)
    m, z, h, q = place.here()
    flat = green0.reshape(1, local, 2 * orbitals, orbitals)
    groups = ((0, local // 2), (local // 2, local))
    stay = place.shifts[0]
    last_made = []

    def cut_and_send(part):
        mine = cut_call(place, part, flat, last_made)
        last_made[:] = [mine[0]]
        return [
            piece if shift == stay else lax.ppermute(piece, AXES, place.shift_perm(shift))
            for shift, piece in zip(place.shifts, mine, strict=True)
        ]

    def send_halos(mine):
        halos = halo_call(place, mine, last_made)
        last_made[:] = [halos[0]]
        return list(mine) + [lax.ppermute(x, AXES, place.plane_perm(odd)) for odd, x in enumerate(halos)]

    back = [[] for _ in groups]

    def partial_sums(inputs):
        addends = []
        for dq in range(1, place.reach):
            (sums,) = smooth_call(mix[dq], inputs, [], 1, last_made)
            last_made[:] = [sums]
            addends.append(lax.ppermute(sums, AXES, place.swap_perm(dq)))
        return addends

    def send_back(part, mixed, group):
        last_made[:] = [mixed[0]]
        arrived = []
        for shift, piece in zip(place.shifts, mixed, strict=True):
            if shift != stay:
                piece = lax.ppermute(piece, AXES, place.shift_perm(shift))
            arrived.append(piece)
            for g in range(len(groups)):
                if group in (g, None):
                    back[g].append((part, shift, piece, group is None))
        return arrived[1:]

    parts = place.parts
    pieces = [cut_and_send(part) for part in parts]
    mix = mixing(place, coupling, shift_table, offsets, last_made)
    last_made[:] = [mix[0]]
    inputs = [send_halos(mine) for mine in pieces]
    last_made[:] = [gate_call(HALO, last_made)]
    sent = []
    for part, mine in zip(parts, inputs, strict=True):
        addends = partial_sums(mine)
        (own,) = smooth_call(mix[0], mine, [], 1, last_made)
        if part != parts[-1]:
            sent = send_back(part, add_call(place, [own, *addends], local, [own]), None)
            continue
        last_made[:] = [gate_call(GATE, [own, *sent])]
        rest, *lead = add_call(place, [own, *addends], groups[0][1], last_made)
        send_back(part, lead, 0)
        send_back(part, part_call(place, rest, last_made), 1)
    out = None
    for (first, last), arrived in zip(groups, back, strict=True):
        out = dyson_call(place, green0, phonon_me, arrived, first, last, out)
    return out


def solution(mesh):
    in_specs = (P("mom", "en", None, None, None), P(), P(), P(), P())
    out_specs = P("mom", "en", None, None, None)
    return jax.shard_map(
        per_device, mesh=mesh, in_specs=in_specs, out_specs=out_specs, check_vma=False
    )
```
